32 devices in a mesh: parts: 2 (over y), gx: 16 (over z, x, core).
Axes of the slice: x: 2, y: 2, z: 4, core: 2. Of those that a mesh axis runs over, the one named last changes fastest.
Arguments:
- e_start: float32 [3, 256, 16, 128], P(None, ('parts', 'gx')), parts along dimension 1, may hold values from -6 to 6
- h_start: float32 [3, 256, 16, 128], P(None, ('parts', 'gx')), parts along dimension 1, may hold values from -6 to 6
- background: float32 [256, 16, 128], P(('parts', 'gx')), parts along dimension 0, may hold values from 1 to 4
- design: float32 [256, 16, 128], P(('parts', 'gx')), parts along dimension 0, may hold values from -6 to 6
- design_mask: int32 [256, 16, 128], P(('parts', 'gx')), parts along dimension 0, may hold values 0 or 1
- plane_counts: int32 [32], P(('parts', 'gx')), parts along dimension 0, may hold values from 1 to 8, 32 in all
- plane_rows: int32 [32, 8], P(('parts', 'gx')), parts along dimension 0, may hold values from 0 to 7, as said below
- source_cells: int32 [128], P('parts'), parts along dimension 0, may hold values from 0 to 262143
- source_amp: float32 [128], P('parts'), parts along dimension 0, may hold values from -8 to 8
- target: float32 [16, 128], replicated, may hold values from 0.1 to 1
Outputs:
- new_design: float32 [256, 16, 128], P(('parts', 'gx')), parts along dimension 0
- final_field: float32 [3, 256, 16, 128], P(None, ('parts', 'gx')), parts along dimension 1
- far_intensity: float32 [32, 128], P('parts'), parts along dimension 0
The draws below stay inside these ranges and needn't reach their ends.
There are 2 independent parts, one for each index of `parts`. The reference program is written for one: setup_inputs(seed, part) draws one part's arguments, and reference() takes and returns one part's arrays. A program takes and returns all parts, laid end to end along the dimension named above; an argument that names none is the same for every part. Nothing has to cross between parts.
Inputs may be any that keep to these rules, and one draw needn't show every extreme that they name: Block d holds plane_counts[d] monitor planes; the counts sum to 32. `plane_rows`: each row holds 8 distinct local row numbers; slot s of block d is a monitor plane when s < plane_counts[d].
All inputs are finite; a program needn't handle non-finite values. No bound on the sum of `design_mask` on one device may be relied on, other than what follows from the above.
Results may differ from the reference program's by a relative error of at most 0.0003.
Values sent between devices are 32-bit elements; how exact they have to be, the bound alone decides.
A program may use at most 64 MiB of HBM per device.

```python
import math
import jax
import jax.numpy as jnp
import numpy as np
from jax import lax

CX = 8
NY = 128
NZ = 16
STEPS = 8
ITERS = 2
KY = 128
KZ = 16
MOST = 8
BLOCKS = 16
NX = 128
MON = 32
SRC = 64


def draw_plane_rows(key, part):
    key = jax.random.fold_in(key, 7)
    scores = jax.random.randint(key, (BLOCKS, CX), 0, 1 << 20) * CX + jnp.arange(CX, dtype=jnp.int32)[None, :]
    order = jnp.argsort(scores, axis=1, stable=True)
    return order[:, :MOST].astype(jnp.int32)


def with_ends(drawn, stream_key, smallest, largest):
    longest = drawn.shape.index(max(drawn.shape))
    spots = []
    for shift in (0, 1):
        where = [jax.random.randint(jax.random.fold_in(stream_key, axis), (), 0, length) for axis, length in enumerate(drawn.shape)]
        where[longest] = (where[longest] + shift) % drawn.shape[longest]
        spots.append(tuple(where))
    return drawn.at[spots[0]].set(smallest).at[spots[1]].set(largest)


def levels(stream_key, extent, shards, smallest, largest):
    factor_of, own = 1.0, jax.random.fold_in(stream_key, 6)
    for position, blocks in shards:
        steps = jnp.exp(jax.random.uniform(jax.random.fold_in(own, position), (blocks,), jnp.float32, smallest / len(shards), largest / len(shards)))
        factor_of = factor_of * jnp.repeat(steps, extent[position] // blocks).reshape([-1 if axis == position else 1 for axis in range(len(extent))])
    return factor_of


def profile(amount, total, most, slope):
    portions = [(1 << 20) // math.isqrt(rank ** slope) + 1 for rank in range(2, amount + 1)]
    rest, counts = total - most - (amount - 1), [1] * (amount - 1)
    while rest > 0:
        movable = [i for i in range(amount - 1) if counts[i] < most]
        mass, remaining = sum([portions[i] for i in movable]), rest
        for i in movable:
            extra = min(most - counts[i], max(1, remaining * portions[i] // mass), rest)
            counts[i] = counts[i] + extra
            rest = rest - extra
    return np.array([most] + counts)


def uneven_parts(stream_key, count, total, most, lean):
    if count == 2:
        one = jax.random.randint(stream_key, (), max(1, total - most), min(most, total - 1) + 1)
        return jnp.stack([one, total - one])
    sizes = jnp.asarray(profile(count, total, most, lean), jnp.int32)
    pairs = (count - 1) // 2
    source_of, taker = sizes[1:1 + 2 * pairs:2], sizes[2:2 + 2 * pairs:2]
    margin = jnp.minimum(source_of - 1, most - taker)
    passed = jax.random.randint(jax.random.fold_in(stream_key, 1), (pairs,), 0, 1 << 20) % (margin + 1)
    sizes = sizes.at[1:1 + 2 * pairs:2].set(source_of - passed).at[2:2 + 2 * pairs:2].set(taker + passed)
    return sizes[jax.random.permutation(jax.random.fold_in(stream_key, 2), count)]


def gaussian(rng, extent, spread, most, shards=(), held_as=jnp.bfloat16):
    entries = spread * jax.random.normal(rng, extent, jnp.float32)
    if shards:
        entries = entries * levels(rng, extent, shards, -0.22, 0.18)
    return jnp.clip(entries, -most, most).astype(held_as)


def setup_inputs(seed: int = 0, part: int = 0) -> dict:
    arg_keys = jax.random.split(jax.random.key(seed), 11)
    own_keys = jax.random.split(jax.random.fold_in(arg_keys[10], part), 11)
    return {
        "e_start": gaussian(own_keys[0], (3, NX, NZ, NY), 1.0, 6.0, ((1, 16),), jnp.float32),
        "h_start": gaussian(own_keys[1], (3, NX, NZ, NY), 1.0, 6.0, ((1, 16),), jnp.float32),
        "background": jnp.clip(jnp.exp(math.log(4.0) - 1.3862944 * jax.random.uniform(own_keys[2], (NX, NZ, NY), jnp.float32) ** levels(own_keys[2], (NX, NZ, NY), ((0, 16),), -0.2, 0.2)), 1.0, 4.0),
        "design": gaussian(own_keys[3], (NX, NZ, NY), 1.5, 6.0, ((0, 16),), jnp.float32),
        "design_mask": with_ends((jax.random.randint(own_keys[4], (NX, NZ, NY), 0, 2) < 1).astype(jnp.int32), jax.random.fold_in(own_keys[4], 1), 0, 1),
        "plane_counts": uneven_parts(own_keys[5], BLOCKS, MON, MOST, 2).astype(jnp.int32),
        "plane_rows": draw_plane_rows(jax.random.fold_in(jax.random.fold_in(arg_keys[10], part), 71), part),
        "source_cells": with_ends(jax.random.randint(own_keys[7], (SRC,), 0, NX * NZ * NY), jax.random.fold_in(own_keys[7], 1), 0, (NX * NZ * NY) - 1).astype(jnp.int32),
        "source_amp": gaussian(own_keys[8], (SRC,), 2.0, 8.0, (), jnp.float32),
        "target": jnp.clip(jnp.exp(jax.random.uniform(arg_keys[9], (KZ, KY), jnp.float32, math.log(0.1), math.log(1.0))), 0.1, 1.0),
    }


COURANT = 0.5
OMEGA = 0.7
SPAN_EPS = 8.0
RATE = 0.5
EPSILON = 1e-06
HIGH = lax.Precision.HIGHEST

def forward_diff(field, axis):
    length = field.shape[axis]
    edge = jnp.zeros_like(lax.slice_in_dim(field, 0, 1, axis=axis))
    return jnp.concatenate([lax.slice_in_dim(field, 1, length, axis=axis), edge], axis=axis) - field

def backward_diff(field, axis):
    length = field.shape[axis]
    edge = jnp.zeros_like(lax.slice_in_dim(field, 0, 1, axis=axis))
    return field - jnp.concatenate([edge, lax.slice_in_dim(field, 0, length - 1, axis=axis)], axis=axis)

def update_h(electric, magnetic, after):
    curl_x = forward_diff(electric[2], 2) - forward_diff(electric[1], 1)
    curl_y = forward_diff(electric[0], 1) - (jnp.concatenate([electric[2][1:], after[1]], axis=0) - electric[2])
    curl_z = jnp.concatenate([electric[1][1:], after[0]], axis=0) - electric[1] - forward_diff(electric[0], 2)
    return jnp.stack([magnetic[0] - COURANT * curl_x, magnetic[1] - COURANT * curl_y, magnetic[2] - COURANT * curl_z])

def update_e(electric, magnetic, inverse, before, drive, time_value):
    curl_x = backward_diff(magnetic[2], 2) - backward_diff(magnetic[1], 1)
    curl_y = backward_diff(magnetic[0], 1) - (magnetic[2] - jnp.concatenate([before[1], magnetic[2][:-1]], axis=0))
    curl_z = magnetic[1] - jnp.concatenate([before[0], magnetic[1][:-1]], axis=0) - backward_diff(magnetic[0], 2)
    parts = [electric[0] + COURANT * inverse * curl_x, electric[1] + COURANT * inverse * curl_y, electric[2] + COURANT * inverse * curl_z]
    for component, kind, source in drive:
        factor = math.cos(OMEGA * time_value) if kind == 'cos' else math.sin(OMEGA * time_value)
        parts[component] = parts[component] + factor * source
    return jnp.stack(parts)

def angle_tables(width_y, depth_z):
    angle = (jnp.arange(KY, dtype=jnp.float32) + 0.5) * (math.pi / (2 * KY))
    wavenumber = OMEGA / COURANT
    wave_y = wavenumber * jnp.sin(angle)
    wave_x = wavenumber * jnp.cos(angle)
    wave_z = (jnp.arange(KZ, dtype=jnp.float32) + 0.5) * (math.pi / KZ)
    phase_y = jnp.arange(width_y, dtype=jnp.float32)[:, None] * wave_y[None, :]
    cos_y = jnp.cos(phase_y)
    sin_y = jnp.sin(phase_y)
    to_far = jnp.concatenate([jnp.concatenate([cos_y, -sin_y], axis=1), jnp.concatenate([sin_y, cos_y], axis=1)], axis=0)
    to_near = jnp.concatenate([jnp.concatenate([cos_y.T, -sin_y.T], axis=1), jnp.concatenate([sin_y.T, cos_y.T], axis=1)], axis=0)
    phase_z = jnp.arange(depth_z, dtype=jnp.float32)[:, None] * wave_z[None, :]
    return (to_far, to_near, jnp.cos(phase_z), jnp.sin(phase_z), wave_x)

def project(near_re, near_im, plane_x, tables):
    to_far, to_near, cos_z, sin_z, wave_x = tables
    stacked = jnp.concatenate([near_re, near_im], axis=-1)
    flat = jnp.dot(stacked.reshape(-1, stacked.shape[-1]), to_far, precision=HIGH, preferred_element_type=jnp.float32)
    along_y = flat.reshape(stacked.shape[:-1] + (to_far.shape[1],))
    part_re = along_y[..., :KY]
    part_im = along_y[..., KY:]
    zed_re = jnp.einsum('fszk,zm->fsmk', part_re, cos_z, precision=HIGH) + jnp.einsum('fszk,zm->fsmk', part_im, sin_z, precision=HIGH)
    zed_im = jnp.einsum('fszk,zm->fsmk', part_im, cos_z, precision=HIGH) - jnp.einsum('fszk,zm->fsmk', part_re, sin_z, precision=HIGH)
    phase_x = plane_x[:, None] * wave_x[None, :]
    cos_x = jnp.cos(phase_x)[None, :, None, :]
    sin_x = jnp.sin(phase_x)[None, :, None, :]
    return (lax.optimization_barrier(jnp.sum(cos_x * zed_re + sin_x * zed_im, axis=1)), lax.optimization_barrier(jnp.sum(cos_x * zed_im - sin_x * zed_re, axis=1)))

def back_project(weight_re, weight_im, plane_x, tables):
    to_far, to_near, cos_z, sin_z, wave_x = tables
    phase_x = plane_x[:, None] * wave_x[None, :]
    cos_x = jnp.cos(phase_x)[None, :, None, :]
    sin_x = jnp.sin(phase_x)[None, :, None, :]
    slot_re = cos_x * weight_re[:, None] + sin_x * weight_im[:, None]
    slot_im = cos_x * weight_im[:, None] - sin_x * weight_re[:, None]
    zed_re = jnp.einsum('fsmk,zm->fszk', slot_re, cos_z, precision=HIGH) + jnp.einsum('fsmk,zm->fszk', slot_im, sin_z, precision=HIGH)
    zed_im = jnp.einsum('fsmk,zm->fszk', slot_im, cos_z, precision=HIGH) - jnp.einsum('fsmk,zm->fszk', slot_re, sin_z, precision=HIGH)
    stacked = jnp.concatenate([zed_re, zed_im], axis=-1)
    flat = jnp.dot(stacked.reshape(-1, stacked.shape[-1]), to_near, precision=HIGH, preferred_element_type=jnp.float32)
    near = flat.reshape(stacked.shape[:-1] + (to_near.shape[1],))
    half = to_near.shape[1] // 2
    return (near[..., :half], near[..., half:])

def reference(e_start, h_start, background, design, design_mask, plane_counts, plane_rows, source_cells, source_amp, target):
    cells = NX * NZ * NY
    source_field = jnp.zeros((cells,), jnp.float32).at[source_cells].add(source_amp).reshape(NX, NZ, NY)
    mask_float = design_mask.astype(jnp.float32)
    slot_rows = (jnp.arange(BLOCKS, dtype=jnp.int32)[:, None] * CX + plane_rows).reshape(-1).astype(jnp.int32)
    slot_valid = (jnp.arange(MOST, dtype=jnp.int32)[None, :] < plane_counts[:, None]).astype(jnp.float32).reshape(-1)
    valid_four = slot_valid[None, :, None, None]
    plane_x = slot_rows.astype(jnp.float32)
    tables = angle_tables(NY, NZ)
    far_scale = 1.0 / math.sqrt(NY * NZ * MON * STEPS)
    near_scale = 1.0 / math.sqrt(KY * KZ)
    edge = jnp.zeros((2, 1, NZ, NY), jnp.float32)
    current = design
    electric = e_start
    intensity = jnp.zeros((KZ, KY), jnp.float32)
    for iteration in range(ITERS):
        squash = jax.nn.sigmoid(current)
        inverse = 1.0 / (background + SPAN_EPS * mask_float * squash)
        electric, magnetic = (e_start, h_start)
        history = []
        monitor_re = jnp.zeros((2, slot_rows.shape[0], NZ, NY), jnp.float32)
        monitor_im = jnp.zeros((2, slot_rows.shape[0], NZ, NY), jnp.float32)
        drive = [(2, 'sin', source_field)]
        for time_value in range(1, STEPS + 1):
            magnetic = update_h(electric, magnetic, edge)
            electric = update_e(electric, magnetic, inverse, edge, drive, time_value)
            history.append(electric)
            plane = jnp.stack([jnp.take(electric[1], slot_rows, axis=0) + jnp.take(magnetic[2], slot_rows, axis=0), jnp.take(electric[2], slot_rows, axis=0) - jnp.take(magnetic[1], slot_rows, axis=0)])
            monitor_re = monitor_re + math.cos(OMEGA * time_value) * plane
            monitor_im = monitor_im - math.sin(OMEGA * time_value) * plane
        far_re, far_im = project(monitor_re * valid_four, monitor_im * valid_four, plane_x, tables)
        far_re = far_re * far_scale
        far_im = far_im * far_scale
        weight_re = 2.0 * target * far_re
        weight_im = -2.0 * target * far_im
        intensity = lax.optimization_barrier(jnp.sum(far_re * far_re + far_im * far_im, axis=0))
        back_re, back_im = back_project(weight_re, weight_im, plane_x, tables)
        back_re = back_re * near_scale * valid_four
        back_im = back_im * near_scale * valid_four
        dense = jnp.zeros((2, 2, NX, NZ, NY), jnp.float32).at[:, :, slot_rows].add(jnp.stack([back_re, back_im], axis=1))
        back_drive = [(1, 'cos', dense[0, 0]), (1, 'sin', dense[0, 1]), (2, 'cos', dense[1, 0]), (2, 'sin', dense[1, 1])]
        back_electric = jnp.zeros_like(e_start)
        back_magnetic = jnp.zeros_like(h_start)
        sensitivity = jnp.zeros((NX, NZ, NY), jnp.float32)
        for count in range(STEPS):
            time_value = STEPS - count
            back_magnetic = update_h(back_electric, back_magnetic, edge)
            back_electric = update_e(back_electric, back_magnetic, inverse, edge, back_drive, time_value)
            sensitivity = sensitivity + lax.optimization_barrier(jnp.sum(history[time_value - 1] * back_electric, axis=0))
        gradient = sensitivity * mask_float * SPAN_EPS * squash * (1.0 - squash)
        total = jnp.sum(gradient * gradient)
        current = current + RATE * gradient / jnp.sqrt(total / (NX * NZ * NY) + EPSILON)
    return (current, electric, intensity)
```

```python
import functools
import math

import jax
import jax.numpy as jnp
import ml_dtypes
import numpy as np
from jax import lax
from jax.experimental import pallas as pl
from jax.experimental.pallas import tpu as pltpu
from jax.sharding import PartitionSpec as P

STEPS = 8
ITERS = 2
KY = 128
KZ = 16
PLANES_DEV = 2
COURANT = 0.5
OMEGA = 0.7
SPAN_EPS = 8.0
RATE = 0.5
EPSILON = 1e-06
HIGH = lax.Precision.HIGHEST
MESH = pl.DeviceIdType.MESH
GROUP = 16
CH = 4
F32 = jnp.float32


def split_table(table):
    high = table.astype(ml_dtypes.bfloat16)
    low = (table - high.astype(np.float64)).astype(ml_dtypes.bfloat16)
    return np.stack([high, low])


def make_tables(width, depth, rows, devices):
    angle = (np.arange(KY) + 0.5) * (math.pi / (2 * KY))
    wave_y = OMEGA / COURANT * np.sin(angle)
    wave_x = OMEGA / COURANT * np.cos(angle)
    wave_z = (np.arange(KZ) + 0.5) * (math.pi / KZ)
    phase_y = np.arange(width)[:, None] * wave_y[None, :]
    c, s = np.cos(phase_y), np.sin(phase_y)
    to_far = np.block([[c, -s], [s, c]])
    to_near = np.block([[c.T, -s.T], [s.T, c.T]])
    phase_z = wave_z[:, None] * np.arange(depth)[None, :]
    c, s = np.cos(phase_z), np.sin(phase_z)
    z_far = np.block([[c, s], [-s, c]])
    z_near = np.block([[c.T, s.T], [-s.T, c.T]])
    base = rows * np.arange(devices)[:, None] * wave_x[None, :]
    local = np.arange(-rows, 2 * rows)[:, None] * wave_x[None, :]
    times = np.arange(STEPS + 1) * OMEGA
    return (
        split_table(to_far),
        split_table(to_near),
        np.stack([z_far, z_near]).astype(np.float32),
        np.stack([np.cos(base), np.sin(base)]).astype(np.float32),
        np.stack([np.cos(local), np.sin(local)]).astype(np.float32),
        np.stack([np.cos(times), np.sin(times)]).astype(np.float32),
    )


def split(value):
    high = value.astype(jnp.bfloat16)
    return high, (value - high.astype(F32)).astype(jnp.bfloat16)


def dot3(left, table):
    high, low = split(left)
    out = jnp.dot(low, table[0], preferred_element_type=F32)
    out = out + jnp.dot(high, table[1], preferred_element_type=F32)
    return out + jnp.dot(high, table[0], preferred_element_type=F32)


def kernel(
    n, rows, depth, far_scale, near_scale, cells_total,
    e_in, h_in, bg_in, de_in, ma_in, counts, slots, cells, amps, target,
    to_far, to_near, z_tab, x_base, x_local, time_tab,
    new_out, final_out, far_out,
    eh, hh, bg, de, ma, marks, inv, src, ae, ah, adj, sens, grads, phase,
    part, gathered, reduced, crossed, summed, norms, norm_cross, mine,
    local_sem, halo_send, halo_recv, grad_send, grad_recv,
    rs_send, rs_recv, ag_send, ag_recv, no_send, no_recv, x_send, x_recv, xn_send, xn_recv,
):
    me = lax.axis_index("gx")
    own_part = lax.axis_index("parts")
    groups = n // GROUP
    loc = lax.rem(me, GROUP)
    grp = me // GROUP
    first = grp * GROUP
    block = rows * depth
    wide = 3 * block
    width = bg_in.shape[-1]
    has_left = me > 0
    has_right = me < n - 1
    OWN = pl.ds(block, block)
    ghost = (pl.ds(0, block), pl.ds(2 * block, block))

    def device(index):
        return (own_part, index)

    barrier = pltpu.get_barrier_semaphore()
    for d in range(1, GROUP):
        pl.semaphore_signal(
            barrier, inc=1, device_id=device(first + lax.rem(loc + d, GROUP)), device_id_type=MESH
        )
    for d in range(1, groups):
        pl.semaphore_signal(
            barrier, inc=1, device_id=device(lax.rem(me + d * GROUP, n)), device_id_type=MESH
        )
    greetings = GROUP - 1 + groups - 1
    if groups > 1:
        outer_left = has_left & (loc == 0)
        outer_right = has_right & (loc == GROUP - 1)

        @pl.when(outer_left)
        def _():
            pl.semaphore_signal(barrier, inc=1, device_id=device(me - 1), device_id_type=MESH)

        @pl.when(outer_right)
        def _():
            pl.semaphore_signal(barrier, inc=1, device_id=device(me + 1), device_id_type=MESH)

        greetings = greetings + outer_left.astype(jnp.int32) + outer_right.astype(jnp.int32)

    moves = [
        pltpu.make_async_copy(e_in, eh.at[0, :, OWN], local_sem.at[0]),
        pltpu.make_async_copy(h_in, hh.at[0, :, OWN], local_sem.at[1]),
        pltpu.make_async_copy(bg_in, bg.at[OWN], local_sem.at[2]),
        pltpu.make_async_copy(de_in, de.at[OWN], local_sem.at[3]),
        pltpu.make_async_copy(ma_in, ma.at[OWN], local_sem.at[4]),
    ]
    for move in moves:
        move.start()

    row_of = lax.broadcasted_iota(jnp.int32, (rows, width), 0)
    mark = jnp.zeros((rows, width), F32)
    for s in range(slots.shape[1]):
        mark = mark + jnp.where((row_of == slots[0, s]) & (s < counts[0]), 1.0, 0.0)
    marks[1] = mark

    pl.semaphore_wait(barrier, greetings)

    def halo(side):
        other = device(jnp.clip(me + (1 if side == 0 else -1), 0, n - 1))
        where = ghost[side]
        pairs = [
            (e_in, eh.at[0, :, where]),
            (h_in, hh.at[0, :, where]),
            (bg_in, bg.at[where]),
            (de_in, de.at[where]),
            (ma_in, ma.at[where]),
            (marks.at[1], marks.at[2 * side]),
        ]
        return [
            pltpu.make_async_remote_copy(
                src_ref=a, dst_ref=b, send_sem=halo_send.at[side, i], recv_sem=halo_recv.at[side, i],
                device_id=other, device_id_type=MESH,
            )
            for i, (a, b) in enumerate(pairs)
        ]

    def grad_halo(side):
        other = device(jnp.clip(me + (1 if side == 0 else -1), 0, n - 1))
        return pltpu.make_async_remote_copy(
            src_ref=grads.at[OWN], dst_ref=grads.at[ghost[side]],
            send_sem=grad_send.at[side], recv_sem=grad_recv.at[side],
            device_id=other, device_id_type=MESH,
        )

    sends = (has_right, has_left)
    comes = (has_left, has_right)
    for side in (0, 1):

        @pl.when(sends[side])
        def _():
            for copy in halo(side):
                copy.start()

        @pl.when(jnp.logical_not(comes[side]))
        def _():
            where = ghost[side]
            eh[0, :, where] = jnp.zeros((3, block, width), F32)
            hh[0, :, where] = jnp.zeros((3, block, width), F32)
            bg[where] = jnp.ones((block, width), F32)
            de[where] = jnp.zeros((block, width), F32)
            ma[where] = jnp.zeros((block, width), jnp.int32)
            marks[2 * side] = jnp.zeros((rows, width), F32)
            grads[where] = jnp.zeros((block, width), F32)

    ids = cells[...] - (me - 1) * block * width
    line = lax.broadcasted_iota(jnp.int32, (wide, ids.shape[1]), 0)
    lane = lax.broadcasted_iota(jnp.int32, (width, ids.shape[1]), 0)
    place = lax.shift_right_arithmetic(ids, width.bit_length() - 1)
    rest = jnp.bitwise_and(ids, width - 1)
    left = jnp.where(line == place, amps[...], 0.0)
    right = jnp.where(lane == rest, 1.0, 0.0)
    src[...] = lax.dot_general(
        left, right, (((1,), (1,)), ((), ())), precision=HIGH, preferred_element_type=F32
    )

    base_c, base_s = x_base[0, pl.ds(me, 1), :], x_base[1, pl.ds(me, 1), :]
    phase[0] = base_c * x_local[0] - base_s * x_local[1]
    phase[1] = base_s * x_local[0] + base_c * x_local[1]

    for move in moves:
        move.wait()
    for side in (0, 1):

        @pl.when(comes[side])
        def _():
            for copy in halo(side):
                copy.wait_recv()

    span = CH * depth
    y_at = lax.broadcasted_iota(jnp.int32, (span, width), 1)
    z_at = lax.rem(lax.broadcasted_iota(jnp.int32, (span, width), 0), depth)
    y_last, y_first = y_at == width - 1, y_at == 0
    z_last, z_first = z_at == depth - 1, z_at == 0

    def up_y(f):
        return jnp.where(y_last, 0.0, pltpu.roll(f, width - 1, 1)) - f

    def up_z(f):
        return jnp.where(z_last, 0.0, pltpu.roll(f, span - 1, 0)) - f

    def down_y(f):
        return f - jnp.where(y_first, 0.0, pltpu.roll(f, 1, 1))

    def down_z(f):
        return f - jnp.where(z_first, 0.0, pltpu.roll(f, 1, 0))

    def behind(edge, f):
        return jnp.concatenate([edge, f[: span - depth]], axis=0)

    def sweep(t, load_e, load_h, store_e, store_h, drive):
        chunks = 3 * rows // CH

        def chunk(c, carry):
            prev_y, prev_z = carry
            at = pl.ds(pl.multiple_of(c * span, span), span)
            ahead = pl.ds(pl.multiple_of(c * span + depth, depth), span)
            ch = jnp.where(has_left | (c >= rows // CH), COURANT, 0.0).astype(F32)
            ex, ey, ez = (load_e(i, at) for i in range(3))
            hx = load_h(0, at) - ch * (up_y(ez) - up_z(ey))
            hy = load_h(1, at) - ch * (up_z(ex) - (load_e(2, ahead) - ez))
            hz = load_h(2, at) - ch * ((load_e(1, ahead) - ey) - up_y(ex))
            store_h(0, at, hx)
            store_h(1, at, hy)
            store_h(2, at, hz)
            scale = inv[at]
            add_y, add_z = drive(at)
            nx = ex + scale * (down_y(hz) - down_z(hy))
            ny = ey + scale * (down_z(hx) - (hz - behind(prev_z, hz)))
            nz = ez + scale * ((hy - behind(prev_y, hy)) - down_y(hx)) + add_z
            if add_y is not None:
                ny = ny + add_y
            store_e(0, at, nx)
            store_e(1, at, ny)
            store_e(2, at, nz)
            return hy[span - depth :], hz[span - depth :]

        low = (t - 1) // CH
        high = (3 * rows - t + CH - 1) // CH
        zero = jnp.zeros((depth, width), F32)
        lax.fori_loop(low, jnp.minimum(high, chunks), chunk, (zero, zero))

    def forward(t, _):
        def load(ref):
            return lambda i, at: ref[t - 1, i, at]

        def store(ref):
            def put(i, at, value):
                ref[t, i, at] = value

            return put

        wave = time_tab[1, t]
        sweep(t, load(eh), load(hh), store(eh), store(hh), lambda at: (None, wave * src[at]))
        return 0

    def adjoint(tau, _):
        t = STEPS + 1 - tau
        cos_t, sin_t = time_tab[0, t], time_tab[1, t]

        def load(ref):
            return lambda i, at: ref[i, at]

        def store(ref):
            def put(i, at, value):
                ref[i, at] = value

            return put

        def drive(at):
            return tuple(cos_t * adj[2 * f, at] + sin_t * adj[2 * f + 1, at] for f in (0, 1))

        sweep(tau, load(ae), load(ah), store(ae), store(ah), drive)
        add_sensitivity(t)
        return 0

    def add_sensitivity(t):
        for c in range(rows // CH):
            at, here = pl.ds(c * span, span), pl.ds(block + c * span, span)
            total = sens[at]
            for i in range(3):
                total = total + eh[t, i, here] * ae[i, here]
            sens[at] = total

    def peers(copy_of):
        return [copy_of(lax.rem(loc + d, GROUP), d) for d in range(1, GROUP)]

    def remote(src_ref, dst_ref, send, recv, target_device):
        return pltpu.make_async_remote_copy(
            src_ref=src_ref, dst_ref=dst_ref, send_sem=send, recv_sem=recv,
            device_id=device(target_device), device_id_type=MESH,
        )

    def exchange(out, landing):
        for copy in out:
            copy.start()
        for copy in landing:
            copy.wait_recv()
        for copy in out:
            copy.wait_send()

    def across(value, buffer, send, recv):
        if groups == 1:
            return value
        buffer[grp] = value
        out = [
            remote(buffer.at[grp], buffer.at[grp], send.at[d], recv.at[grp], lax.rem(me + d * GROUP, n))
            for d in range(1, groups)
        ]
        landing = []
        for d in range(1, groups):
            there = lax.rem(grp + d, groups)
            landing.append(remote(buffer.at[there], buffer.at[there], send.at[d], recv.at[there], me))
        exchange(out, landing)
        total = buffer[0]
        for g in range(1, groups):
            total = total + buffer[g]
        return total

    def reduce_far():
        out = peers(lambda p, d: remote(part.at[p], reduced.at[loc], rs_send.at[d], rs_recv.at[loc], first + p))
        landing = peers(lambda p, d: remote(part.at[p], reduced.at[p], rs_send.at[d], rs_recv.at[p], first + p))
        reduced[loc] = part[loc]
        exchange(out, landing)
        total = reduced[0]
        for i in range(1, GROUP):
            total = total + reduced[i]
        gathered[loc] = across(total, crossed, x_send, x_recv)
        out = peers(lambda p, d: remote(gathered.at[loc], gathered.at[loc], ag_send.at[d], ag_recv.at[loc], first + p))
        landing = peers(lambda p, d: remote(gathered.at[p], gathered.at[p], ag_send.at[d], ag_recv.at[p], first + p))
        exchange(out, landing)

    def reduce_norm(tile):
        norms[loc] = tile
        out = peers(lambda p, d: remote(norms.at[loc], norms.at[loc], no_send.at[d], no_recv.at[loc], first + p))
        landing = peers(lambda p, d: remote(norms.at[p], norms.at[p], no_send.at[d], no_recv.at[p], first + p))
        exchange(out, landing)
        total = norms[0]
        for i in range(1, GROUP):
            total = total + norms[i]
        total = across(total, norm_cross, xn_send, xn_recv)
        return jnp.sum(jnp.sum(total, axis=0, keepdims=True), axis=1, keepdims=True)

    lines = KZ // 4
    for iteration in range(ITERS):
        last = iteration == ITERS - 1
        for c in range(3):
            at = pl.ds(c * block, block)
            squash = 1.0 / (1.0 + jnp.exp(-de[at]))
            scale = COURANT / (bg[at] + SPAN_EPS * ma[at].astype(F32) * squash)
            if c != 1:
                scale = jnp.where(comes[0] if c == 0 else comes[1], scale, 0.0)
            inv[at] = scale
        lax.fori_loop(1, STEPS + 1, forward, 0)
        if last:
            final = pltpu.make_async_copy(eh.at[STEPS, :, OWN], final_out, local_sem.at[0])
            final.start()

        for f in (0, 1):
            far_re = jnp.zeros((depth, KY), F32)
            far_im = jnp.zeros((depth, KY), F32)
            re_rows, im_rows = [], []
            for r in range(rows):
                at = pl.ds(block + r * depth, depth)
                mon_re = jnp.zeros((depth, width), F32)
                mon_im = jnp.zeros((depth, width), F32)
                for t in range(1, STEPS + 1):
                    plane = eh[t, 1, at] + hh[t, 2, at] if f == 0 else eh[t, 2, at] - hh[t, 1, at]
                    mon_re = mon_re + math.cos(OMEGA * t) * plane
                    mon_im = mon_im - math.sin(OMEGA * t) * plane
                re_rows.append(mon_re)
                im_rows.append(mon_im)
            stacked = jnp.concatenate(
                [jnp.concatenate(re_rows, axis=0), jnp.concatenate(im_rows, axis=0)], axis=1
            )
            flat = dot3(stacked, to_far)
            for r in range(rows):
                valid = marks[1, r : r + 1, :]
                cos_x = phase[0, rows + r : rows + r + 1, :] * valid
                sin_x = phase[1, rows + r : rows + r + 1, :] * valid
                y_re = flat[r * depth : (r + 1) * depth, :KY]
                y_im = flat[r * depth : (r + 1) * depth, KY:]
                far_re = far_re + cos_x * y_re + sin_x * y_im
                far_im = far_im + cos_x * y_im - sin_x * y_re
            far = far_scale * jnp.dot(
                z_tab[0], jnp.concatenate([far_re, far_im], axis=0), precision=HIGH, preferred_element_type=F32
            )
            for i in range(8):
                part[8 * f + i] = far[lines * i : lines * (i + 1)]
        reduce_far()

        power = jnp.zeros((KZ, KY), F32)
        for f in (0, 1):
            total = jnp.concatenate([gathered[8 * f + i] for i in range(8)], axis=0)
            total_re, total_im = total[:KZ], total[KZ:]
            power = power + total_re * total_re + total_im * total_im
            weight = jnp.concatenate([2.0 * target[...] * total_re, -2.0 * target[...] * total_im], axis=0)
            zed = near_scale * jnp.dot(z_tab[1], weight, precision=HIGH, preferred_element_type=F32)
            zed_re, zed_im = zed[:depth], zed[depth:]
            for side in range(3):
                slot = []
                for r in range(rows):
                    x = side * rows + r
                    valid = marks[side, r : r + 1, :]
                    cos_x = phase[0, x : x + 1, :] * valid
                    sin_x = phase[1, x : x + 1, :] * valid
                    slot.append(
                        jnp.concatenate(
                            [cos_x * zed_re + sin_x * zed_im, cos_x * zed_im - sin_x * zed_re], axis=1
                        )
                    )
                near = dot3(jnp.concatenate(slot, axis=0), to_near)
                at = pl.ds(side * block, block)
                adj[2 * f, at] = near[:, :width]
                adj[2 * f + 1, at] = near[:, width:]
                ae[f + 1, at] = (
                    math.cos(OMEGA * STEPS) * near[:, :width] + math.sin(OMEGA * STEPS) * near[:, width:]
                )
        if last:
            far_out[...] = power
        ae[0] = jnp.zeros(ae.shape[1:], F32)
        ah[...] = jnp.zeros(ah.shape, F32)
        sens[...] = jnp.zeros(sens.shape, F32)
        add_sensitivity(STEPS)
        lax.fori_loop(2, STEPS + 1, adjoint, 0)

        squash = 1.0 / (1.0 + jnp.exp(-de[OWN]))
        gradient = sens[...] * ma[OWN].astype(F32) * SPAN_EPS * squash * (1.0 - squash)
        grads[OWN] = gradient
        if not last:
            for side in (0, 1):

                @pl.when(sends[side])
                def _():
                    grad_halo(side).start()

        square = gradient * gradient
        tile = square[:8]
        for i in range(1, block // 8):
            tile = tile + square[8 * i : 8 * (i + 1)]
        factor = RATE / jnp.sqrt(reduce_norm(tile) / cells_total + EPSILON)
        if last:
            new_out[...] = de[OWN] + factor * gradient
        else:
            for side in (0, 1):

                @pl.when(comes[side])
                def _():
                    grad_halo(side).wait_recv()

            de[...] = de[...] + factor * grads[...]
            for side in (0, 1):

                @pl.when(sends[side])
                def _():
                    grad_halo(side).wait_send()

    for side in (0, 1):

        @pl.when(sends[side])
        def _():
            for copy in halo(side):
                copy.wait_send()

    final.wait()


def body(n, e_start, h_start, background, design, design_mask, plane_counts, plane_rows, source_cells, source_amp, target):
    rows, depth, width = background.shape
    block = rows * depth
    groups = n // GROUP
    tables = make_tables(width, depth, rows, n)
    far_scale = 1.0 / math.sqrt(width * depth * PLANES_DEV * n * STEPS)
    near_scale = 1.0 / math.sqrt(KY * KZ)
    vmem = pl.BlockSpec(memory_space=pltpu.VMEM)
    smem = pl.BlockSpec(memory_space=pltpu.SMEM)
    hbm = pl.BlockSpec(memory_space=pl.ANY)
    dma = pltpu.SemaphoreType.DMA
    fields = (3, 3 * block + depth, width)
    new_design, final_field, intensity = pl.pallas_call(
        functools.partial(
            kernel, n, rows, depth, far_scale, near_scale, float(rows * n * depth * width)
        ),
        out_shape=(
            jax.ShapeDtypeStruct((block, width), F32),
            jax.ShapeDtypeStruct((3, block, width), F32),
            jax.ShapeDtypeStruct((KZ, KY), F32),
        ),
        in_specs=[hbm] * 5 + [smem] * 2 + [vmem] * 8 + [smem],
        out_specs=(vmem, hbm, vmem),
        scratch_shapes=[
            pltpu.VMEM((STEPS + 1,) + fields, F32),
            pltpu.VMEM((STEPS + 1,) + fields, F32),
            pltpu.VMEM((3 * block, width), F32),
            pltpu.VMEM((3 * block, width), F32),
            pltpu.VMEM((3 * block, width), jnp.int32),
            pltpu.VMEM((3, rows, width), F32),
            pltpu.VMEM((3 * block, width), F32),
            pltpu.VMEM((3 * block, width), F32),
            pltpu.VMEM(fields, F32),
            pltpu.VMEM(fields, F32),
            pltpu.VMEM((4, 3 * block, width), F32),
            pltpu.VMEM((block, width), F32),
            pltpu.VMEM((3 * block, width), F32),
            pltpu.VMEM((2, 3 * rows, width), F32),
            pltpu.VMEM((GROUP, KZ // 4, KY), F32),
            pltpu.VMEM((GROUP, KZ // 4, KY), F32),
            pltpu.VMEM((GROUP, KZ // 4, KY), F32),
            pltpu.VMEM((groups, KZ // 4, KY), F32),
            pltpu.VMEM((KZ // 4, KY), F32),
            pltpu.VMEM((GROUP, 8, width), F32),
            pltpu.VMEM((groups, 8, width), F32),
            pltpu.VMEM((8, width), F32),
            dma((5,)),
            dma((2, 6)),
            dma((2, 6)),
            dma((2,)),
            dma((2,)),
        ]
        + [dma((GROUP,))] * 6
        + [dma((groups,))] * 4,
        compiler_params=pltpu.CompilerParams(
            collective_id=0, has_side_effects=True, vmem_limit_bytes=40 * 1024 * 1024
        ),
    )(
        e_start.reshape(3, block, width),
        h_start.reshape(3, block, width),
        background.reshape(block, width),
        design.reshape(block, width),
        design_mask.reshape(block, width),
        plane_counts,
        plane_rows,
        source_cells.reshape(1, -1),
        source_amp.reshape(1, -1),
        target,
        *tables,
    )
    return (
        new_design.reshape(rows, depth, width),
        final_field.reshape(3, rows, depth, width),
        intensity,
    )


def solution(mesh):
    return jax.shard_map(
        functools.partial(body, mesh.shape["gx"]),
        mesh=mesh,
        in_specs=(
            P(None, ("parts", "gx"), None, None),
            P(None, ("parts", "gx"), None, None),
            P(("parts", "gx"), None, None),
            P(("parts", "gx"), None, None),
            P(("parts", "gx"), None, None),
            P(("parts", "gx")),
            P(("parts", "gx"), None),
            P("parts"),
            P("parts"),
            P(),
        ),
        out_specs=(
            P(("parts", "gx"), None, None),
            P(None, ("parts", "gx"), None, None),
            P("parts", None),
        ),
        check_vma=False,
    )
```

```python
import functools
import math

import jax
import jax.numpy as jnp
import ml_dtypes
import numpy as np
from jax import lax
from jax.experimental import pallas as pl
from jax.experimental.pallas import tpu as pltpu
from jax.sharding import PartitionSpec as P

STEPS = 8
ITERS = 2
KY = 128
KZ = 16
PLANES_DEV = 2
COURANT = 0.5
OMEGA = 0.7
SPAN_EPS = 8.0
RATE = 0.5
EPSILON = 1e-06
HIGH = lax.Precision.HIGHEST
MESH = pl.DeviceIdType.MESH
GROUP = 16
CH = 8
F32 = jnp.float32


def split_table(table):
    high = table.astype(ml_dtypes.bfloat16)
    low = (table - high.astype(np.float64)).astype(ml_dtypes.bfloat16)
    return np.stack([high, low])


def make_tables(width, depth, rows, devices):
    angle = (np.arange(KY) + 0.5) * (math.pi / (2 * KY))
    wave_y = OMEGA / COURANT * np.sin(angle)
    wave_x = OMEGA / COURANT * np.cos(angle)
    wave_z = (np.arange(KZ) + 0.5) * (math.pi / KZ)
    phase_y = np.arange(width)[:, None] * wave_y[None, :]
    c, s = np.cos(phase_y), np.sin(phase_y)
    to_far = np.block([[c, -s], [s, c]])
    to_near = np.block([[c.T, -s.T], [s.T, c.T]])
    phase_z = wave_z[:, None] * np.arange(depth)[None, :]
    c, s = np.cos(phase_z), np.sin(phase_z)
    z_far = np.block([[c, s], [-s, c]])
    z_near = np.block([[c.T, s.T], [-s.T, c.T]])
    base = rows * np.arange(devices)[:, None] * wave_x[None, :]
    local = np.arange(-rows, 2 * rows)[:, None] * wave_x[None, :]
    along = np.concatenate([local, base])
    return (
        np.concatenate([split_table(to_far), split_table(to_near)]),
        np.stack([z_far, z_near]).astype(np.float32),
        np.stack([np.cos(along), np.sin(along)]).astype(np.float32),
    )


def at_time(function, t):
    value = jnp.where(t == 1, function(OMEGA), 0.0).astype(F32)
    for k in range(2, STEPS + 1):
        value = jnp.where(t == k, function(OMEGA * k), value).astype(F32)
    return value


def split(value):
    high = value.astype(jnp.bfloat16)
    return high, (value - high.astype(F32)).astype(jnp.bfloat16)


def dot3(left, table, i):
    high, low = split(left)
    out = jnp.dot(low, table[i], preferred_element_type=F32)
    out = out + jnp.dot(high, table[i + 1], preferred_element_type=F32)
    return out + jnp.dot(high, table[i], preferred_element_type=F32)


def kernel(
    n, rows, depth, far_scale, near_scale, cells_total,
    e_in, h_in, bg_in, de_in, ma_in, *rest,
):
    small_in, (new_out, final_out, far_out), rest = rest[:8], rest[8:11], rest[11:]
    small, rest = rest[:8], rest[8:]
    run(
        n, rows, depth, far_scale, near_scale, cells_total, e_in, h_in, bg_in, de_in, ma_in,
        small_in, *small, new_out, final_out, far_out, *rest,
    )


def run(
    n, rows, depth, far_scale, near_scale, cells_total, e_in, h_in, bg_in, de_in, ma_in,
    small_in, counts, slots, cells, amps, target, y_tab, z_tab, x_tab,
    new_out, final_out, far_out,
    eh, hh, bg, de, ma, marks, inv, src, ae, ah, adj, sens, grads, phase,
    part, gathered, reduced, crossed, norms, norm_cross, new_own, power_own,
    local_sem, halo_send, halo_recv, grad_send, grad_recv,
    rs_send, rs_recv, ag_send, ag_recv, no_send, no_recv, x_send, x_recv, xn_send, xn_recv,
):
    me = lax.axis_index("gx")
    own_part = lax.axis_index("parts")
    groups = n // GROUP
    loc = lax.rem(me, GROUP)
    grp = me // GROUP
    first = grp * GROUP
    block = rows * depth
    wide = 3 * block
    width = bg_in.shape[-1]
    has_left = me > 0
    has_right = me < n - 1
    OWN = pl.ds(block, block)
    ghost = (pl.ds(0, block), pl.ds(2 * block, block))

    def device(index):
        return (own_part, index)

    barrier = pltpu.get_barrier_semaphore()
    for d in range(1, GROUP):
        pl.semaphore_signal(
            barrier, inc=1, device_id=device(first + lax.rem(loc + d, GROUP)), device_id_type=MESH
        )
    for d in range(1, groups):
        pl.semaphore_signal(
            barrier, inc=1, device_id=device(lax.rem(me + d * GROUP, n)), device_id_type=MESH
        )
    greetings = GROUP - 1 + groups - 1
    if groups > 1:
        outer_left = has_left & (loc == 0)
        outer_right = has_right & (loc == GROUP - 1)

        @pl.when(outer_left)
        def _():
            pl.semaphore_signal(barrier, inc=1, device_id=device(me - 1), device_id_type=MESH)

        @pl.when(outer_right)
        def _():
            pl.semaphore_signal(barrier, inc=1, device_id=device(me + 1), device_id_type=MESH)

        greetings = greetings + outer_left.astype(jnp.int32) + outer_right.astype(jnp.int32)

    moves = [
        pltpu.make_async_copy(e_in, eh.at[0, :, OWN], local_sem.at[0]),
        pltpu.make_async_copy(h_in, hh.at[0, :, OWN], local_sem.at[1]),
        pltpu.make_async_copy(bg_in, bg.at[OWN], local_sem.at[2]),
        pltpu.make_async_copy(de_in, de.at[OWN], local_sem.at[3]),
        pltpu.make_async_copy(ma_in, ma.at[OWN], local_sem.at[4]),
    ]
    loads = [
        pltpu.make_async_copy(a, b, local_sem.at[5 + i])
        for i, (a, b) in enumerate(zip(small_in, (counts, slots, cells, amps, target, y_tab, z_tab, x_tab)))
    ]
    for move in loads + moves:
        move.start()
    for move in loads:
        move.wait()

    at_row = lax.broadcasted_iota(jnp.int32, (rows, slots.shape[1]), 0)
    at_slot = lax.broadcasted_iota(jnp.int32, (rows, slots.shape[1]), 1)
    hit = jnp.where((at_row == slots[...]) & (at_slot < counts[...]), 1.0, 0.0)
    marks[1] = jnp.broadcast_to(jnp.sum(hit, axis=1, keepdims=True), (rows, width))

    pl.semaphore_wait(barrier, greetings)

    def halo(side):
        other = device(jnp.clip(me + (1 if side == 0 else -1), 0, n - 1))
        where = ghost[side]
        pairs = [
            (e_in, eh.at[0, :, where]),
            (h_in, hh.at[0, :, where]),
            (bg_in, bg.at[where]),
            (de_in, de.at[where]),
            (ma_in, ma.at[where]),
            (marks.at[1], marks.at[2 * side]),
        ]
        return [
            pltpu.make_async_remote_copy(
                src_ref=a, dst_ref=b, send_sem=halo_send.at[side, i], recv_sem=halo_recv.at[side, i],
                device_id=other, device_id_type=MESH,
            )
            for i, (a, b) in enumerate(pairs)
        ]

    def grad_halo(side):
        other = device(jnp.clip(me + (1 if side == 0 else -1), 0, n - 1))
        return pltpu.make_async_remote_copy(
            src_ref=grads.at[OWN], dst_ref=grads.at[ghost[side]],
            send_sem=grad_send.at[side], recv_sem=grad_recv.at[side],
            device_id=other, device_id_type=MESH,
        )

    sends = (has_right, has_left)
    comes = (has_left, has_right)
    for side in (0, 1):

        @pl.when(sends[side])
        def _():
            for copy in halo(side):
                copy.start()

        @pl.when(jnp.logical_not(comes[side]))
        def _():
            where = ghost[side]
            eh[0, :, where] = jnp.zeros((3, block, width), F32)
            hh[0, :, where] = jnp.zeros((3, block, width), F32)
            bg[where] = jnp.ones((block, width), F32)
            de[where] = jnp.zeros((block, width), F32)
            ma[where] = jnp.zeros((block, width), jnp.int32)
            marks[2 * side] = jnp.zeros((rows, width), F32)
            grads[where] = jnp.zeros((block, width), F32)

    ids = cells[...] - (me - 1) * block * width
    line = lax.broadcasted_iota(jnp.int32, (wide, ids.shape[1]), 0)
    lane = lax.broadcasted_iota(jnp.int32, (width, ids.shape[1]), 0)
    place = lax.shift_right_arithmetic(ids, width.bit_length() - 1)
    rest = jnp.bitwise_and(ids, width - 1)
    left = jnp.where(line == place, amps[...], 0.0)
    right = jnp.where(lane == rest, 1.0, 0.0)
    src[...] = lax.dot_general(
        left, right, (((1,), (1,)), ((), ())), precision=HIGH, preferred_element_type=F32
    )

    base_c, base_s = (x_tab[i, pl.ds(3 * rows + me, 1), :] for i in (0, 1))
    near_c, near_s = (x_tab[i, : 3 * rows, :] for i in (0, 1))
    phase[0] = base_c * near_c - base_s * near_s
    phase[1] = base_s * near_c + base_c * near_s

    for move in moves:
        move.wait()
    for side in (0, 1):

        @pl.when(comes[side])
        def _():
            for copy in halo(side):
                copy.wait_recv()

    span = CH * depth
    y_at = lax.broadcasted_iota(jnp.int32, (span, width), 1)
    z_at = lax.rem(lax.broadcasted_iota(jnp.int32, (span, width), 0), depth)
    y_last, y_first = y_at == width - 1, y_at == 0
    z_last, z_first = z_at == depth - 1, z_at == 0

    def up_y(f):
        return jnp.where(y_last, 0.0, pltpu.roll(f, width - 1, 1)) - f

    def up_z(f):
        return jnp.where(z_last, 0.0, pltpu.roll(f, span - 1, 0)) - f

    def down_y(f):
        return f - jnp.where(y_first, 0.0, pltpu.roll(f, 1, 1))

    def down_z(f):
        return f - jnp.where(z_first, 0.0, pltpu.roll(f, 1, 0))

    def behind(edge, f):
        return jnp.concatenate([edge, f[: span - depth]], axis=0)

    def sweep(t, load_e, load_h, store_e, store_h, drive):
        chunks = 3 * rows // CH

        def chunk(c, carry):
            prev_y, prev_z = carry
            at = pl.ds(pl.multiple_of(c * span, span), span)
            ahead = pl.ds(pl.multiple_of(c * span + depth, depth), span)
            ch = jnp.where(has_left | (c >= rows // CH), COURANT, 0.0).astype(F32)
            ex, ey, ez = (load_e(i, at) for i in range(3))
            hx = load_h(0, at) - ch * (up_y(ez) - up_z(ey))
            hy = load_h(1, at) - ch * (up_z(ex) - (load_e(2, ahead) - ez))
            hz = load_h(2, at) - ch * ((load_e(1, ahead) - ey) - up_y(ex))
            store_h(0, at, hx)
            store_h(1, at, hy)
            store_h(2, at, hz)
            scale = inv[at]
            add_y, add_z = drive(at)
            nx = ex + scale * (down_y(hz) - down_z(hy))
            ny = ey + scale * (down_z(hx) - (hz - behind(prev_z, hz)))
            nz = ez + scale * ((hy - behind(prev_y, hy)) - down_y(hx)) + add_z
            if add_y is not None:
                ny = ny + add_y
            store_e(0, at, nx)
            store_e(1, at, ny)
            store_e(2, at, nz)
            return hy[span - depth :], hz[span - depth :]

        low = (t - 1) // CH
        high = (3 * rows - t + CH - 1) // CH
        zero = jnp.zeros((depth, width), F32)
        lax.fori_loop(low, jnp.minimum(high, chunks), chunk, (zero, zero))

    def forward(t, _):
        def load(ref):
            return lambda i, at: ref[t - 1, i, at]

        def store(ref):
            def put(i, at, value):
                ref[t, i, at] = value

            return put

        wave = at_time(math.sin, t)
        sweep(t, load(eh), load(hh), store(eh), store(hh), lambda at: (None, wave * src[at]))
        return 0

    def adjoint(tau, _):
        t = STEPS + 1 - tau
        cos_t, sin_t = at_time(math.cos, t), at_time(math.sin, t)

        def load(ref):
            return lambda i, at: ref[i, at]

        def store(ref):
            def put(i, at, value):
                ref[i, at] = value

            return put

        def drive(at):
            return tuple(cos_t * adj[2 * f, at] + sin_t * adj[2 * f + 1, at] for f in (0, 1))

        sweep(tau, load(ae), load(ah), store(ae), store(ah), drive)
        add_sensitivity(t)
        return 0

    def add_sensitivity(t):
        for c in range(rows // CH):
            at, here = pl.ds(c * span, span), pl.ds(block + c * span, span)
            total = sens[at]
            for i in range(3):
                total = total + eh[t, i, here] * ae[i, here]
            sens[at] = total

    def peers(copy_of):
        return [copy_of(lax.rem(loc + d, GROUP), d) for d in range(1, GROUP)]

    def remote(src_ref, dst_ref, send, recv, target_device):
        return pltpu.make_async_remote_copy(
            src_ref=src_ref, dst_ref=dst_ref, send_sem=send, recv_sem=recv,
            device_id=device(target_device), device_id_type=MESH,
        )

    def exchange(out, landing):
        for copy in out:
            copy.start()
        for copy in landing:
            copy.wait_recv()
        pending.extend(out)

    pending = []

    def settle():
        for copy in pending:
            copy.wait_send()
        pending.clear()

    def across(value, buffer, send, recv):
        if groups == 1:
            return value
        buffer[grp] = value
        out = [
            remote(buffer.at[grp], buffer.at[grp], send.at[d], recv.at[grp], lax.rem(me + d * GROUP, n))
            for d in range(1, groups)
        ]
        landing = []
        for d in range(1, groups):
            there = lax.rem(grp + d, groups)
            landing.append(remote(buffer.at[there], buffer.at[there], send.at[d], recv.at[there], me))
        exchange(out, landing)
        total = buffer[0]
        for g in range(1, groups):
            total = total + buffer[g]
        return total

    def reduce_far():
        out = peers(lambda p, d: remote(part.at[p], reduced.at[loc], rs_send.at[d], rs_recv.at[loc], first + p))
        landing = peers(lambda p, d: remote(part.at[p], reduced.at[p], rs_send.at[d], rs_recv.at[p], first + p))
        reduced[loc] = part[loc]
        exchange(out, landing)
        total = reduced[0]
        for i in range(1, GROUP):
            total = total + reduced[i]
        gathered[loc] = across(total, crossed, x_send, x_recv)
        out = peers(lambda p, d: remote(gathered.at[loc], gathered.at[loc], ag_send.at[d], ag_recv.at[loc], first + p))
        landing = peers(lambda p, d: remote(gathered.at[p], gathered.at[p], ag_send.at[d], ag_recv.at[p], first + p))
        exchange(out, landing)

    def reduce_norm(tile):
        norms[loc] = tile
        out = peers(lambda p, d: remote(norms.at[loc], norms.at[loc], no_send.at[d], no_recv.at[loc], first + p))
        landing = peers(lambda p, d: remote(norms.at[p], norms.at[p], no_send.at[d], no_recv.at[p], first + p))
        exchange(out, landing)
        total = norms[0]
        for i in range(1, GROUP):
            total = total + norms[i]
        total = across(total, norm_cross, xn_send, xn_recv)
        return jnp.sum(jnp.sum(total, axis=0, keepdims=True), axis=1, keepdims=True)

    lines = KZ // 4
    results = []
    for iteration in range(ITERS):
        last = iteration == ITERS - 1
        for c in range(3):
            at = pl.ds(c * block, block)
            squash = 1.0 / (1.0 + jnp.exp(-de[at]))
            scale = COURANT / (bg[at] + SPAN_EPS * ma[at].astype(F32) * squash)
            if c != 1:
                scale = jnp.where(comes[0] if c == 0 else comes[1], scale, 0.0)
            inv[at] = scale
        lax.fori_loop(1, STEPS + 1, forward, 0)
        if last:
            results.append(pltpu.make_async_copy(eh.at[STEPS, :, OWN], final_out, local_sem.at[0]))
            results[-1].start()

        for f in (0, 1):
            far_re = jnp.zeros((depth, KY), F32)
            far_im = jnp.zeros((depth, KY), F32)
            re_rows, im_rows = [], []
            for r in range(rows):
                at = pl.ds(block + r * depth, depth)
                mon_re = jnp.zeros((depth, width), F32)
                mon_im = jnp.zeros((depth, width), F32)
                for t in range(1, STEPS + 1):
                    plane = eh[t, 1, at] + hh[t, 2, at] if f == 0 else eh[t, 2, at] - hh[t, 1, at]
                    mon_re = mon_re + math.cos(OMEGA * t) * plane
                    mon_im = mon_im - math.sin(OMEGA * t) * plane
                re_rows.append(mon_re)
                im_rows.append(mon_im)
            stacked = jnp.concatenate(
                [jnp.concatenate(re_rows, axis=0), jnp.concatenate(im_rows, axis=0)], axis=1
            )
            flat = dot3(stacked, y_tab, 0)
            for r in range(rows):
                valid = marks[1, r : r + 1, :]
                cos_x = phase[0, rows + r : rows + r + 1, :] * valid
                sin_x = phase[1, rows + r : rows + r + 1, :] * valid
                y_re = flat[r * depth : (r + 1) * depth, :KY]
                y_im = flat[r * depth : (r + 1) * depth, KY:]
                far_re = far_re + cos_x * y_re + sin_x * y_im
                far_im = far_im + cos_x * y_im - sin_x * y_re
            far = far_scale * jnp.dot(
                z_tab[0], jnp.concatenate([far_re, far_im], axis=0), precision=HIGH, preferred_element_type=F32
            )
            for i in range(8):
                part[8 * f + i] = far[lines * i : lines * (i + 1)]
        reduce_far()

        power = jnp.zeros((KZ, KY), F32)
        for f in (0, 1):
            total = jnp.concatenate([gathered[8 * f + i] for i in range(8)], axis=0)
            total_re, total_im = total[:KZ], total[KZ:]
            power = power + total_re * total_re + total_im * total_im
            weight = jnp.concatenate([2.0 * target[...] * total_re, -2.0 * target[...] * total_im], axis=0)
            zed = near_scale * jnp.dot(z_tab[1], weight, precision=HIGH, preferred_element_type=F32)
            zed_re, zed_im = zed[:depth], zed[depth:]
            for side in range(3):
                slot = []
                for r in range(rows):
                    x = side * rows + r
                    valid = marks[side, r : r + 1, :]
                    cos_x = phase[0, x : x + 1, :] * valid
                    sin_x = phase[1, x : x + 1, :] * valid
                    slot.append(
                        jnp.concatenate(
                            [cos_x * zed_re + sin_x * zed_im, cos_x * zed_im - sin_x * zed_re], axis=1
                        )
                    )
                near = dot3(jnp.concatenate(slot, axis=0), y_tab, 2)
                at = pl.ds(side * block, block)
                adj[2 * f, at] = near[:, :width]
                adj[2 * f + 1, at] = near[:, width:]
                ae[f + 1, at] = (
                    math.cos(OMEGA * STEPS) * near[:, :width] + math.sin(OMEGA * STEPS) * near[:, width:]
                )
        if last:
            power_own[...] = power
            results.append(pltpu.make_async_copy(power_own, far_out, local_sem.at[2]))
            results[-1].start()
        ae[0] = jnp.zeros(ae.shape[1:], F32)
        ah[...] = jnp.zeros(ah.shape, F32)
        sens[...] = jnp.zeros(sens.shape, F32)
        add_sensitivity(STEPS)
        lax.fori_loop(2, STEPS + 1, adjoint, 0)
        settle()

        squash = 1.0 / (1.0 + jnp.exp(-de[OWN]))
        gradient = sens[...] * ma[OWN].astype(F32) * SPAN_EPS * squash * (1.0 - squash)
        grads[OWN] = gradient
        if not last:
            for side in (0, 1):

                @pl.when(sends[side])
                def _():
                    grad_halo(side).start()

        square = gradient * gradient
        tile = square[:8]
        for i in range(1, block // 8):
            tile = tile + square[8 * i : 8 * (i + 1)]
        factor = RATE / jnp.sqrt(reduce_norm(tile) / cells_total + EPSILON)
        if last:
            new_own[...] = de[OWN] + factor * gradient
            results.append(pltpu.make_async_copy(new_own, new_out, local_sem.at[1]))
            results[-1].start()
            settle()
        else:
            for side in (0, 1):

                @pl.when(comes[side])
                def _():
                    grad_halo(side).wait_recv()

            de[...] = de[...] + factor * grads[...]
            settle()
            for side in (0, 1):

                @pl.when(sends[side])
                def _():
                    grad_halo(side).wait_send()

    for side in (0, 1):

        @pl.when(sends[side])
        def _():
            for copy in halo(side):
                copy.wait_send()

    for move in results:
        move.wait()


def body(n, e_start, h_start, background, design, design_mask, plane_counts, plane_rows, source_cells, source_amp, target):
    rows, depth, width = background.shape
    block = rows * depth
    groups = n // GROUP
    small = [
        plane_counts.reshape(1, 1),
        plane_rows,
        source_cells.reshape(1, -1),
        source_amp.reshape(1, -1),
        target,
        *make_tables(width, depth, rows, n),
    ]
    far_scale = 1.0 / math.sqrt(width * depth * PLANES_DEV * n * STEPS)
    near_scale = 1.0 / math.sqrt(KY * KZ)
    hbm = pl.BlockSpec(memory_space=pltpu.HBM)
    dma = pltpu.SemaphoreType.DMA
    fields = (3, 3 * block + depth, width)
    new_design, final_field, intensity = pl.pallas_call(
        functools.partial(
            kernel, n, rows, depth, far_scale, near_scale, float(rows * n * depth * width)
        ),
        out_shape=(
            jax.ShapeDtypeStruct((block, width), F32),
            jax.ShapeDtypeStruct((3, block, width), F32),
            jax.ShapeDtypeStruct((KZ, KY), F32),
        ),
        in_specs=[hbm] * 13,
        out_specs=(hbm,) * 3,
        scratch_shapes=[pltpu.VMEM(a.shape, a.dtype) for a in small]
        + [
            pltpu.VMEM((STEPS + 1,) + fields, F32),
            pltpu.VMEM((STEPS + 1,) + fields, F32),
            pltpu.VMEM((3 * block, width), F32),
            pltpu.VMEM((3 * block, width), F32),
            pltpu.VMEM((3 * block, width), jnp.int32),
            pltpu.VMEM((3, rows, width), F32),
            pltpu.VMEM((3 * block, width), F32),
            pltpu.VMEM((3 * block, width), F32),
            pltpu.VMEM(fields, F32),
            pltpu.VMEM(fields, F32),
            pltpu.VMEM((4, 3 * block, width), F32),
            pltpu.VMEM((block, width), F32),
            pltpu.VMEM((3 * block, width), F32),
            pltpu.VMEM((2, 3 * rows, width), F32),
            pltpu.VMEM((GROUP, KZ // 4, KY), F32),
            pltpu.VMEM((GROUP, KZ // 4, KY), F32),
            pltpu.VMEM((GROUP, KZ // 4, KY), F32),
            pltpu.VMEM((groups, KZ // 4, KY), F32),
            pltpu.VMEM((GROUP, 8, width), F32),
            pltpu.VMEM((groups, 8, width), F32),
            pltpu.VMEM((block, width), F32),
            pltpu.VMEM((KZ, KY), F32),
            dma((13,)),
            dma((2, 6)),
            dma((2, 6)),
            dma((2,)),
            dma((2,)),
        ]
        + [dma((GROUP,))] * 6
        + [dma((groups,))] * 4,
        compiler_params=pltpu.CompilerParams(
            collective_id=0, has_side_effects=True, vmem_limit_bytes=64 * 1024 * 1024
        ),
    )(
        e_start.reshape(3, block, width),
        h_start.reshape(3, block, width),
        background.reshape(block, width),
        design.reshape(block, width),
        design_mask.reshape(block, width),
        *small,
    )
    return (
        new_design.reshape(rows, depth, width),
        final_field.reshape(3, rows, depth, width),
        intensity,
    )


def solution(mesh):
    return jax.shard_map(
        functools.partial(body, mesh.shape["gx"]),
        mesh=mesh,
        in_specs=(
            P(None, ("parts", "gx"), None, None),
            P(None, ("parts", "gx"), None, None),
            P(("parts", "gx"), None, None),
            P(("parts", "gx"), None, None),
            P(("parts", "gx"), None, None),
            P(("parts", "gx")),
            P(("parts", "gx"), None),
            P("parts"),
            P("parts"),
            P(),
        ),
        out_specs=(
            P(("parts", "gx"), None, None),
            P(None, ("parts", "gx"), None, None),
            P("parts", None),
        ),
        check_vma=False,
    )
```

```python
import functools
import math

import jax
import jax.numpy as jnp
import ml_dtypes
import numpy as np
from jax import lax
from jax.experimental import pallas as pl
from jax.experimental.pallas import tpu as pltpu
from jax.sharding import PartitionSpec as P

STEPS = 8
ITERS = 2
KY = 128
KZ = 16
PLANES_DEV = 2
COURANT = 0.5
OMEGA = 0.7
SPAN_EPS = 8.0
RATE = 0.5
EPSILON = 1e-06
HIGH = lax.Precision.HIGHEST
MESH = pl.DeviceIdType.MESH
GROUP = 16
CH = 8
F32 = jnp.float32


def split_table(table):
    high = table.astype(ml_dtypes.bfloat16)
    low = (table - high.astype(np.float64)).astype(ml_dtypes.bfloat16)
    return np.stack([high, low])


def make_tables(width, depth, rows, devices):
    angle = (np.arange(KY) + 0.5) * (math.pi / (2 * KY))
    wave_y = OMEGA / COURANT * np.sin(angle)
    wave_x = OMEGA / COURANT * np.cos(angle)
    wave_z = (np.arange(KZ) + 0.5) * (math.pi / KZ)
    phase_y = np.arange(width)[:, None] * wave_y[None, :]
    c, s = np.cos(phase_y), np.sin(phase_y)
    to_far = np.block([[c, -s], [s, c]])
    to_near = np.block([[c.T, -s.T], [s.T, c.T]])
    phase_z = wave_z[:, None] * np.arange(depth)[None, :]
    c, s = np.cos(phase_z), np.sin(phase_z)
    z_far = np.block([[c, s], [-s, c]])
    z_near = np.block([[c.T, s.T], [-s.T, c.T]])
    base = rows * np.arange(devices)[:, None] * wave_x[None, :]
    local = np.arange(-rows, 2 * rows)[:, None] * wave_x[None, :]
    along = np.concatenate([local, base])
    return (
        np.concatenate([split_table(to_far), split_table(to_near)]),
        np.stack([z_far, z_near]).astype(np.float32),
        np.stack([np.cos(along), np.sin(along)]).astype(np.float32),
    )


def at_time(function, t):
    value = jnp.where(t == 1, function(OMEGA), 0.0).astype(F32)
    for k in range(2, STEPS + 1):
        value = jnp.where(t == k, function(OMEGA * k), value).astype(F32)
    return value


def split(value):
    high = value.astype(jnp.bfloat16)
    return high, (value - high.astype(F32)).astype(jnp.bfloat16)


def dot3(left, table, i):
    high, low = split(left)
    out = jnp.dot(low, table[i], preferred_element_type=F32)
    out = out + jnp.dot(high, table[i + 1], preferred_element_type=F32)
    return out + jnp.dot(high, table[i], preferred_element_type=F32)


def kernel(
    n, rows, depth, far_scale, near_scale, cells_total,
    e_in, h_in, bg_in, de_in, ma_in, *rest,
):
    small_in, (new_out, final_out, far_out), rest = rest[:8], rest[8:11], rest[11:]
    small, rest = rest[:8], rest[8:]
    run(
        n, rows, depth, far_scale, near_scale, cells_total, e_in, h_in, bg_in, de_in, ma_in,
        small_in, *small, new_out, final_out, far_out, *rest,
    )


def run(
    n, rows, depth, far_scale, near_scale, cells_total, e_in, h_in, bg_in, de_in, ma_in,
    small_in, counts, slots, cells, amps, target, y_tab, z_tab, x_tab,
    new_out, final_out, far_out,
    eh, hh, bg, de, ma, marks, inv, src, ae, ah, adj, sens, grads, phase,
    part, gathered, reduced, crossed, norms, norm_cross, new_own, power_own,
    local_sem, halo_send, halo_recv, grad_send, grad_recv,
    rs_send, rs_recv, ag_send, ag_recv, no_send, no_recv, x_send, x_recv, xn_send, xn_recv,
):
    me = lax.axis_index("gx")
    own_part = lax.axis_index("parts")
    groups = n // GROUP
    loc = lax.rem(me, GROUP)
    grp = me // GROUP
    first = grp * GROUP
    block = rows * depth
    wide = 3 * block
    width = bg_in.shape[-1]
    has_left = me > 0
    has_right = me < n - 1
    OWN = pl.ds(block, block)
    ghost = (pl.ds(0, block), pl.ds(2 * block, block))

    def device(index):
        return (own_part, index)

    barrier = pltpu.get_barrier_semaphore()
    for d in range(1, GROUP):
        pl.semaphore_signal(
            barrier, inc=1, device_id=device(first + lax.rem(loc + d, GROUP)), device_id_type=MESH
        )
    for d in range(1, groups):
        pl.semaphore_signal(
            barrier, inc=1, device_id=device(lax.rem(me + d * GROUP, n)), device_id_type=MESH
        )
    greetings = GROUP - 1 + groups - 1
    if groups > 1:
        outer_left = has_left & (loc == 0)
        outer_right = has_right & (loc == GROUP - 1)

        @pl.when(outer_left)
        def _():
            pl.semaphore_signal(barrier, inc=1, device_id=device(me - 1), device_id_type=MESH)

        @pl.when(outer_right)
        def _():
            pl.semaphore_signal(barrier, inc=1, device_id=device(me + 1), device_id_type=MESH)

        greetings = greetings + outer_left.astype(jnp.int32) + outer_right.astype(jnp.int32)

    moves = [
        pltpu.make_async_copy(e_in, eh.at[0, :, OWN], local_sem.at[0]),
        pltpu.make_async_copy(h_in, hh.at[0, :, OWN], local_sem.at[1]),
        pltpu.make_async_copy(bg_in, bg.at[OWN], local_sem.at[2]),
        pltpu.make_async_copy(de_in, de.at[OWN], local_sem.at[3]),
        pltpu.make_async_copy(ma_in, ma.at[OWN], local_sem.at[4]),
    ]
    loads = [
        pltpu.make_async_copy(a, b, local_sem.at[5 + i])
        for i, (a, b) in enumerate(zip(small_in, (counts, slots, cells, amps, target, y_tab, z_tab, x_tab)))
    ]
    for move in loads + moves:
        move.start()
    for move in loads:
        move.wait()

    at_row = lax.broadcasted_iota(jnp.int32, (rows, slots.shape[1]), 0)
    at_slot = lax.broadcasted_iota(jnp.int32, (rows, slots.shape[1]), 1)
    hit = jnp.where((at_row == slots[...]) & (at_slot < counts[...]), 1.0, 0.0)
    marks[1] = jnp.broadcast_to(jnp.sum(hit, axis=1, keepdims=True), (rows, width))

    for move in moves[2:]:
        move.wait()

    def set_inverse(at, inside=None):
        squash = 1.0 / (1.0 + jnp.exp(-de[at]))
        scale = COURANT / (bg[at] + SPAN_EPS * ma[at].astype(F32) * squash)
        inv[at] = scale if inside is None else jnp.where(inside, scale, 0.0)

    set_inverse(OWN)
    pl.semaphore_wait(barrier, greetings)

    def halo(side, early):
        other = device(jnp.clip(me + (1 if side == 0 else -1), 0, n - 1))
        where = ghost[side]
        pairs = [
            (e_in, eh.at[0, :, where]),
            (h_in, hh.at[0, :, where]),
            (bg_in, bg.at[where]),
            (de_in, de.at[where]),
            (ma_in, ma.at[where]),
            (marks.at[1], marks.at[2 * side]),
            (inv.at[OWN], inv.at[where]),
        ]
        taken = (0, 1, 6) if early else (2, 3, 4, 5)
        return [
            pltpu.make_async_remote_copy(
                src_ref=a, dst_ref=b, send_sem=halo_send.at[side, i], recv_sem=halo_recv.at[side, i],
                device_id=other, device_id_type=MESH,
            )
            for i, (a, b) in enumerate(pairs)
            if i in taken
        ]

    def grad_halo(side):
        other = device(jnp.clip(me + (1 if side == 0 else -1), 0, n - 1))
        return pltpu.make_async_remote_copy(
            src_ref=grads.at[OWN], dst_ref=grads.at[ghost[side]],
            send_sem=grad_send.at[side], recv_sem=grad_recv.at[side],
            device_id=other, device_id_type=MESH,
        )

    sends = (has_right, has_left)
    comes = (has_left, has_right)
    for side in (0, 1):

        @pl.when(sends[side])
        def _():
            for copy in halo(side, True):
                copy.start()

        @pl.when(jnp.logical_not(comes[side]))
        def _():
            where = ghost[side]
            eh[0, :, where] = jnp.zeros((3, block, width), F32)
            hh[0, :, where] = jnp.zeros((3, block, width), F32)
            inv[where] = jnp.zeros((block, width), F32)
            bg[where] = jnp.ones((block, width), F32)
            de[where] = jnp.zeros((block, width), F32)
            ma[where] = jnp.zeros((block, width), jnp.int32)
            marks[2 * side] = jnp.zeros((rows, width), F32)
            grads[where] = jnp.zeros((block, width), F32)

    ids = cells[...] - (me - 1) * block * width
    line = lax.broadcasted_iota(jnp.int32, (wide, ids.shape[1]), 0)
    lane = lax.broadcasted_iota(jnp.int32, (width, ids.shape[1]), 0)
    place = lax.shift_right_arithmetic(ids, width.bit_length() - 1)
    rest = jnp.bitwise_and(ids, width - 1)
    left = jnp.where(line == place, amps[...], 0.0)
    right = jnp.where(lane == rest, 1.0, 0.0)
    src[...] = lax.dot_general(
        left, right, (((1,), (1,)), ((), ())), precision=HIGH, preferred_element_type=F32
    )

    base_c, base_s = (x_tab[i, pl.ds(3 * rows + me, 1), :] for i in (0, 1))
    near_c, near_s = (x_tab[i, : 3 * rows, :] for i in (0, 1))
    phase[0] = base_c * near_c - base_s * near_s
    phase[1] = base_s * near_c + base_c * near_s

    for move in moves[:2]:
        move.wait()
    for side in (0, 1):

        @pl.when(comes[side])
        def _():
            for copy in halo(side, True):
                copy.wait_recv()

    for side in (0, 1):

        @pl.when(sends[side])
        def _():
            for copy in halo(side, False):
                copy.start()

    span = CH * depth
    y_at = lax.broadcasted_iota(jnp.int32, (span, width), 1)
    z_at = lax.rem(lax.broadcasted_iota(jnp.int32, (span, width), 0), depth)
    y_last, y_first = y_at == width - 1, y_at == 0
    z_last, z_first = z_at == depth - 1, z_at == 0

    def up_y(f):
        return jnp.where(y_last, 0.0, pltpu.roll(f, width - 1, 1)) - f

    def up_z(f):
        return jnp.where(z_last, 0.0, pltpu.roll(f, span - 1, 0)) - f

    def down_y(f):
        return f - jnp.where(y_first, 0.0, pltpu.roll(f, 1, 1))

    def down_z(f):
        return f - jnp.where(z_first, 0.0, pltpu.roll(f, 1, 0))

    def behind(edge, f):
        return jnp.concatenate([edge, f[: span - depth]], axis=0)

    def sweep(t, load_e, load_h, store_e, store_h, drive):
        chunks = 3 * rows // CH

        def chunk(c, carry):
            prev_y, prev_z = carry
            at = pl.ds(pl.multiple_of(c * span, span), span)
            ahead = pl.ds(pl.multiple_of(c * span + depth, depth), span)
            ch = jnp.where(has_left | (c >= rows // CH), COURANT, 0.0).astype(F32)
            ex, ey, ez = (load_e(i, at) for i in range(3))
            hx = load_h(0, at) - ch * (up_y(ez) - up_z(ey))
            hy = load_h(1, at) - ch * (up_z(ex) - (load_e(2, ahead) - ez))
            hz = load_h(2, at) - ch * ((load_e(1, ahead) - ey) - up_y(ex))
            store_h(0, at, hx)
            store_h(1, at, hy)
            store_h(2, at, hz)
            scale = inv[at]
            add_y, add_z = drive(at)
            nx = ex + scale * (down_y(hz) - down_z(hy))
            ny = ey + scale * (down_z(hx) - (hz - behind(prev_z, hz)))
            nz = ez + scale * ((hy - behind(prev_y, hy)) - down_y(hx)) + add_z
            if add_y is not None:
                ny = ny + add_y
            store_e(0, at, nx)
            store_e(1, at, ny)
            store_e(2, at, nz)
            return hy[span - depth :], hz[span - depth :]

        low = (t - 1) // CH
        high = (3 * rows - t + CH - 1) // CH
        zero = jnp.zeros((depth, width), F32)
        lax.fori_loop(low, jnp.minimum(high, chunks), chunk, (zero, zero))

    def forward(t, _):
        def load(ref):
            return lambda i, at: ref[t - 1, i, at]

        def store(ref):
            def put(i, at, value):
                ref[t, i, at] = value

            return put

        wave = at_time(math.sin, t)
        sweep(t, load(eh), load(hh), store(eh), store(hh), lambda at: (None, wave * src[at]))
        return 0

    def adjoint(tau, _):
        t = STEPS + 1 - tau
        cos_t, sin_t = at_time(math.cos, t), at_time(math.sin, t)

        def load(ref):
            return lambda i, at: ref[i, at]

        def store(ref):
            def put(i, at, value):
                ref[i, at] = value

            return put

        def drive(at):
            return tuple(cos_t * adj[2 * f, at] + sin_t * adj[2 * f + 1, at] for f in (0, 1))

        sweep(tau, load(ae), load(ah), store(ae), store(ah), drive)
        add_sensitivity(t)
        return 0

    def add_sensitivity(t):
        for c in range(rows // CH):
            at, here = pl.ds(c * span, span), pl.ds(block + c * span, span)
            total = sens[at]
            for i in range(3):
                total = total + eh[t, i, here] * ae[i, here]
            sens[at] = total

    def peers(copy_of):
        return [copy_of(lax.rem(loc + d, GROUP), d) for d in range(1, GROUP)]

    def remote(src_ref, dst_ref, send, recv, target_device):
        return pltpu.make_async_remote_copy(
            src_ref=src_ref, dst_ref=dst_ref, send_sem=send, recv_sem=recv,
            device_id=device(target_device), device_id_type=MESH,
        )

    def exchange(out, landing):
        for copy in out:
            copy.start()
        for copy in landing:
            copy.wait_recv()
        pending.extend(out)

    pending = []

    def settle():
        for copy in pending:
            copy.wait_send()
        pending.clear()

    def across(value, buffer, send, recv):
        if groups == 1:
            return value
        buffer[grp] = value
        out = [
            remote(buffer.at[grp], buffer.at[grp], send.at[d], recv.at[grp], lax.rem(me + d * GROUP, n))
            for d in range(1, groups)
        ]
        landing = []
        for d in range(1, groups):
            there = lax.rem(grp + d, groups)
            landing.append(remote(buffer.at[there], buffer.at[there], send.at[d], recv.at[there], me))
        exchange(out, landing)
        total = buffer[0]
        for g in range(1, groups):
            total = total + buffer[g]
        return total

    def reduce_far():
        out = peers(lambda p, d: remote(part.at[p], reduced.at[loc], rs_send.at[d], rs_recv.at[loc], first + p))
        landing = peers(lambda p, d: remote(part.at[p], reduced.at[p], rs_send.at[d], rs_recv.at[p], first + p))
        reduced[loc] = part[loc]
        exchange(out, landing)
        total = reduced[0]
        for i in range(1, GROUP):
            total = total + reduced[i]
        gathered[loc] = across(total, crossed, x_send, x_recv)
        out = peers(lambda p, d: remote(gathered.at[loc], gathered.at[loc], ag_send.at[d], ag_recv.at[loc], first + p))
        landing = peers(lambda p, d: remote(gathered.at[p], gathered.at[p], ag_send.at[d], ag_recv.at[p], first + p))
        exchange(out, landing)

    def reduce_norm(tile):
        norms[loc] = tile
        out = peers(lambda p, d: remote(norms.at[loc], norms.at[loc], no_send.at[d], no_recv.at[loc], first + p))
        landing = peers(lambda p, d: remote(norms.at[p], norms.at[p], no_send.at[d], no_recv.at[p], first + p))
        exchange(out, landing)
        total = norms[0]
        for i in range(1, GROUP):
            total = total + norms[i]
        total = across(total, norm_cross, xn_send, xn_recv)
        return jnp.sum(jnp.sum(total, axis=0, keepdims=True), axis=1, keepdims=True)

    lines = KZ // 4
    results = []
    for iteration in range(ITERS):
        last = iteration == ITERS - 1
        if iteration > 0:
            set_inverse(ghost[0], comes[0])
            set_inverse(OWN)
            set_inverse(ghost[1], comes[1])
        lax.fori_loop(1, STEPS + 1, forward, 0)
        if last:
            results.append(pltpu.make_async_copy(eh.at[STEPS, :, OWN], final_out, local_sem.at[0]))
            results[-1].start()

        for f in (0, 1):
            far_re = jnp.zeros((depth, KY), F32)
            far_im = jnp.zeros((depth, KY), F32)
            re_rows, im_rows = [], []
            for r in range(rows):
                at = pl.ds(block + r * depth, depth)
                mon_re = jnp.zeros((depth, width), F32)
                mon_im = jnp.zeros((depth, width), F32)
                for t in range(1, STEPS + 1):
                    plane = eh[t, 1, at] + hh[t, 2, at] if f == 0 else eh[t, 2, at] - hh[t, 1, at]
                    mon_re = mon_re + math.cos(OMEGA * t) * plane
                    mon_im = mon_im - math.sin(OMEGA * t) * plane
                re_rows.append(mon_re)
                im_rows.append(mon_im)
            stacked = jnp.concatenate(
                [jnp.concatenate(re_rows, axis=0), jnp.concatenate(im_rows, axis=0)], axis=1
            )
            flat = dot3(stacked, y_tab, 0)
            for r in range(rows):
                valid = marks[1, r : r + 1, :]
                cos_x = phase[0, rows + r : rows + r + 1, :] * valid
                sin_x = phase[1, rows + r : rows + r + 1, :] * valid
                y_re = flat[r * depth : (r + 1) * depth, :KY]
                y_im = flat[r * depth : (r + 1) * depth, KY:]
                far_re = far_re + cos_x * y_re + sin_x * y_im
                far_im = far_im + cos_x * y_im - sin_x * y_re
            far = far_scale * jnp.dot(
                z_tab[0], jnp.concatenate([far_re, far_im], axis=0), precision=HIGH, preferred_element_type=F32
            )
            for i in range(8):
                part[8 * f + i] = far[lines * i : lines * (i + 1)]
        reduce_far()
        if iteration == 0:
            for side in (0, 1):

                @pl.when(comes[side])
                def _():
                    for copy in halo(side, False):
                        copy.wait_recv()

                @pl.when(sends[side])
                def _():
                    for copy in halo(side, True) + halo(side, False):
                        copy.wait_send()

        power = jnp.zeros((KZ, KY), F32)
        for f in (0, 1):
            total = jnp.concatenate([gathered[8 * f + i] for i in range(8)], axis=0)
            total_re, total_im = total[:KZ], total[KZ:]
            power = power + total_re * total_re + total_im * total_im
            weight = jnp.concatenate([2.0 * target[...] * total_re, -2.0 * target[...] * total_im], axis=0)
            zed = near_scale * jnp.dot(z_tab[1], weight, precision=HIGH, preferred_element_type=F32)
            zed_re, zed_im = zed[:depth], zed[depth:]
            for side in range(3):
                slot = []
                for r in range(rows):
                    x = side * rows + r
                    valid = marks[side, r : r + 1, :]
                    cos_x = phase[0, x : x + 1, :] * valid
                    sin_x = phase[1, x : x + 1, :] * valid
                    slot.append(
                        jnp.concatenate(
                            [cos_x * zed_re + sin_x * zed_im, cos_x * zed_im - sin_x * zed_re], axis=1
                        )
                    )
                near = dot3(jnp.concatenate(slot, axis=0), y_tab, 2)
                at = pl.ds(side * block, block)
                adj[2 * f, at] = near[:, :width]
                adj[2 * f + 1, at] = near[:, width:]
                ae[f + 1, at] = (
                    math.cos(OMEGA * STEPS) * near[:, :width] + math.sin(OMEGA * STEPS) * near[:, width:]
                )
        if last:
            power_own[...] = power
            results.append(pltpu.make_async_copy(power_own, far_out, local_sem.at[2]))
            results[-1].start()
        ae[0] = jnp.zeros(ae.shape[1:], F32)
        ah[...] = jnp.zeros(ah.shape, F32)
        sens[...] = jnp.zeros(sens.shape, F32)
        add_sensitivity(STEPS)
        lax.fori_loop(2, STEPS + 1, adjoint, 0)
        settle()

        squash = 1.0 / (1.0 + jnp.exp(-de[OWN]))
        gradient = sens[...] * ma[OWN].astype(F32) * SPAN_EPS * squash * (1.0 - squash)
        grads[OWN] = gradient
        if not last:
            for side in (0, 1):

                @pl.when(sends[side])
                def _():
                    grad_halo(side).start()

        square = gradient * gradient
        tile = square[:8]
        for i in range(1, block // 8):
            tile = tile + square[8 * i : 8 * (i + 1)]
        factor = RATE / jnp.sqrt(reduce_norm(tile) / cells_total + EPSILON)
        if last:
            new_own[...] = de[OWN] + factor * gradient
            results.append(pltpu.make_async_copy(new_own, new_out, local_sem.at[1]))
            results[-1].start()
            settle()
        else:
            for side in (0, 1):

                @pl.when(comes[side])
                def _():
                    grad_halo(side).wait_recv()

            de[...] = de[...] + factor * grads[...]
            settle()
            for side in (0, 1):

                @pl.when(sends[side])
                def _():
                    grad_halo(side).wait_send()

    for move in results:
        move.wait()


def body(n, e_start, h_start, background, design, design_mask, plane_counts, plane_rows, source_cells, source_amp, target):
    rows, depth, width = background.shape
    block = rows * depth
    groups = n // GROUP
    small = [
        plane_counts.reshape(1, 1),
        plane_rows,
        source_cells.reshape(1, -1),
        source_amp.reshape(1, -1),
        target,
        *make_tables(width, depth, rows, n),
    ]
    far_scale = 1.0 / math.sqrt(width * depth * PLANES_DEV * n * STEPS)
    near_scale = 1.0 / math.sqrt(KY * KZ)
    hbm = pl.BlockSpec(memory_space=pltpu.HBM)
    dma = pltpu.SemaphoreType.DMA
    fields = (3, 3 * block + depth, width)
    new_design, final_field, intensity = pl.pallas_call(
        functools.partial(
            kernel, n, rows, depth, far_scale, near_scale, float(rows * n * depth * width)
        ),
        out_shape=(
            jax.ShapeDtypeStruct((block, width), F32),
            jax.ShapeDtypeStruct((3, block, width), F32),
            jax.ShapeDtypeStruct((KZ, KY), F32),
        ),
        in_specs=[hbm] * 13,
        out_specs=(hbm,) * 3,
        scratch_shapes=[pltpu.VMEM(a.shape, a.dtype) for a in small]
        + [
            pltpu.VMEM((STEPS + 1,) + fields, F32),
            pltpu.VMEM((STEPS + 1,) + fields, F32),
            pltpu.VMEM((3 * block, width), F32),
            pltpu.VMEM((3 * block, width), F32),
            pltpu.VMEM((3 * block, width), jnp.int32),
            pltpu.VMEM((3, rows, width), F32),
            pltpu.VMEM((3 * block, width), F32),
            pltpu.VMEM((3 * block, width), F32),
            pltpu.VMEM(fields, F32),
            pltpu.VMEM(fields, F32),
            pltpu.VMEM((4, 3 * block, width), F32),
            pltpu.VMEM((block, width), F32),
            pltpu.VMEM((3 * block, width), F32),
            pltpu.VMEM((2, 3 * rows, width), F32),
            pltpu.VMEM((GROUP, KZ // 4, KY), F32),
            pltpu.VMEM((GROUP, KZ // 4, KY), F32),
            pltpu.VMEM((GROUP, KZ // 4, KY), F32),
            pltpu.VMEM((groups, KZ // 4, KY), F32),
            pltpu.VMEM((GROUP, 8, width), F32),
            pltpu.VMEM((groups, 8, width), F32),
            pltpu.VMEM((block, width), F32),
            pltpu.VMEM((KZ, KY), F32),
            dma((13,)),
            dma((2, 7)),
            dma((2, 7)),
            dma((2,)),
            dma((2,)),
        ]
        + [dma((GROUP,))] * 6
        + [dma((groups,))] * 4,
        compiler_params=pltpu.CompilerParams(
            collective_id=0, has_side_effects=True, vmem_limit_bytes=64 * 1024 * 1024
        ),
    )(
        e_start.reshape(3, block, width),
        h_start.reshape(3, block, width),
        background.reshape(block, width),
        design.reshape(block, width),
        design_mask.reshape(block, width),
        *small,
    )
    return (
        new_design.reshape(rows, depth, width),
        final_field.reshape(3, rows, depth, width),
        intensity,
    )


def solution(mesh):
    return jax.shard_map(
        functools.partial(body, mesh.shape["gx"]),
        mesh=mesh,
        in_specs=(
            P(None, ("parts", "gx"), None, None),
            P(None, ("parts", "gx"), None, None),
            P(("parts", "gx"), None, None),
            P(("parts", "gx"), None, None),
            P(("parts", "gx"), None, None),
            P(("parts", "gx")),
            P(("parts", "gx"), None),
            P("parts"),
            P("parts"),
            P(),
        ),
        out_specs=(
            P(("parts", "gx"), None, None),
            P(None, ("parts", "gx"), None, None),
            P("parts", None),
        ),
        check_vma=False,
    )
```
